32 devices in a mesh: reach: 2 (over y), row: 4 (over z), col: 4 (over x, core).
Axes of the slice: x: 2, y: 2, z: 4, core: 2. Of those that a mesh axis runs over, the one named last changes fastest.
Arguments:
- operator: float32 [2048, 65536], P(('reach', 'col'), 'row'), parts along dimension 0, may hold values from -0.03125 to 0.03125
- basis: float32 [131072, 256], P(('reach', 'row')), parts along dimension 0, may hold values from -6 to 6
Outputs:
- image: float32 [2048, 256], P(('reach', 'row')), parts along dimension 0
The draws below stay inside these ranges and needn't reach their ends.
There are 2 independent parts, one for each index of `reach`. The reference program is written for one: setup_inputs(seed, part) draws one part's arguments, and reference() takes and returns one part's arrays. A program takes and returns all parts, laid end to end along the dimension named above; each array names one. Nothing has to cross between parts.
All inputs are finite; a program needn't handle non-finite values.
Results may differ from the reference program's by a relative error of at most 0.000071.
Values sent between devices are 32-bit elements; how exact they have to be, the bound alone decides.
A program may use at most 64 MiB of HBM per device.

```python
import jax
import jax.numpy as jnp
from jax import lax

NN = 65536
COLS = 256
ROWS = 1024


def strengthened(values, own_key, source, target, blocks, factor):
    owner, partner = [(jnp.arange(values.shape[position]) // (values.shape[position] // blocks)).reshape([-1 if axis == position else 1 for axis in range(values.ndim)]) for position in (source, target)]
    chosen = jax.random.permutation(own_key, blocks)[partner]
    strong = (owner == chosen) | (owner == (partner + blocks // 2) % blocks)
    return jnp.where(strong, factor * values, values)


def level_of(rng, dims, split, low, top_value):
    loudness, own = 1.0, jax.random.fold_in(rng, 6)
    for position, blocks in split:
        heights = jnp.exp(jax.random.uniform(jax.random.fold_in(own, position), (blocks,), jnp.float32, low / len(split), top_value / len(split)))
        loudness = loudness * jnp.repeat(heights, dims[position] // blocks).reshape([-1 if axis == position else 1 for axis in range(len(dims))])
    return loudness


def scatter_about(own_key, shape, width, most, cuts=(), dtype=jnp.bfloat16):
    array = jax.random.normal(own_key, shape, jnp.float32) * width
    if len(cuts) > 0:
        array = level_of(own_key, shape, cuts, -0.22, 0.18) * array
    return jnp.clip(array, min=-most, max=most).astype(dtype)


def gaussian_with(key, extent, scale, reach, shards, heavy, dtype=jnp.bfloat16):
    array = scale * jax.random.normal(key, extent, jnp.float32)
    if shards:
        array = array * level_of(key, extent, shards, -0.22, 0.18)
    return jnp.clip(strengthened(array, jax.random.fold_in(key, 3), *heavy), -reach, reach).astype(dtype)


def setup_inputs(seed: int = 0, part: int = 0) -> dict:
    key_list = jax.random.split(jax.random.key(seed), 3)
    part_splits = jax.random.split(jax.random.fold_in(key_list[2], part), 3)
    operator = gaussian_with(part_splits[0], (ROWS, NN), NN ** -0.5, 0.03125, ((0, 4), (1, 4)), (1, 0, 4, 2.0), jnp.float32)
    basis = scatter_about(part_splits[1], (NN, COLS), 1.0, 6.0, ((0, 4),), jnp.float32)
    return {"operator": operator, "basis": basis}


def reference(operator, basis):
    return jnp.dot(operator, basis, preferred_element_type=jnp.float32, precision=lax.Precision.HIGHEST)
```

```python
import functools

import jax
import jax.numpy as jnp
from jax import lax
from jax.experimental import pallas as pl
from jax.experimental.pallas import tpu as pltpu
from jax.sharding import PartitionSpec as P

MESH = pl.DeviceIdType.MESH
CHUNKS = (64, 64, 64, 64)
TILE = 1024


def split(values):
    high = values.astype(jnp.bfloat16)
    low = (values - high.astype(jnp.float32)).astype(jnp.bfloat16)
    return high, low


def product(a, b_high, b_low):
    rows = a.shape[0]
    high, low = split(a)
    both = jnp.dot(
        jnp.concatenate([high, low], axis=0), b_high, preferred_element_type=jnp.float32
    )
    cross = jnp.dot(high, b_low, preferred_element_type=jnp.float32)
    return both[:rows] + (both[rows:] + cross)


def kernel(
    n_row, n_col, chunks, tile,
    a_hbm, b_hbm, out_ref,
    a_ref, b_ref, b_high, b_low, part, recv,
    a_sem, b_sem, send1, recv1, send2, recv2,
):
    tile_rows, depth = a_hbm.shape
    tiles = depth // tile
    group = n_row // n_col
    out_rows = out_ref.shape[0]
    row, col = lax.axis_index("row"), lax.axis_index("col")
    home = lax.div(row, group) == col
    spans = []
    begin = 0
    for rows in chunks:
        spans.append((begin, rows))
        begin += rows
    compute = spans if group == 1 else [(0, tile_rows)]

    def load_a(index, t):
        start, rows = compute[index]
        here = (pl.ds(start, rows), pl.ds(pl.multiple_of(t * tile, tile), tile))
        return pltpu.make_async_copy(a_hbm.at[here], a_ref.at[here], a_sem.at[index, t])

    def load_b(t):
        here = pl.ds(pl.multiple_of(t * tile, tile), tile)
        return pltpu.make_async_copy(b_hbm.at[here], b_ref.at[here], b_sem.at[t])

    def first_loads(t, _):
        load_b(t).start()
        load_a(0, t).start()
        return 0

    lax.fori_loop(0, tiles, first_loads, 0)

    for index in range(1, len(compute)):
        def later_loads(t, _, index=index):
            load_a(index, t).start()
            return 0

        lax.fori_loop(0, tiles, later_loads, 0)

    barrier = pltpu.get_barrier_semaphore()
    for other in range(n_row):
        @pl.when(jnp.logical_not(home & (row == other)))
        def _(other=other):
            pl.semaphore_signal(
                barrier, inc=1, device_id={"row": other, "col": lax.div(row, group)},
                device_id_type=MESH,
            )
    for step in range(1, n_col):
        pl.semaphore_signal(
            barrier, inc=1, device_id={"row": row, "col": lax.rem(col + step, n_col)},
            device_id_type=MESH,
        )

    def scatter_copy(index, g, k):
        start, rows = spans[index]
        piece = rows // n_col
        return pltpu.make_async_remote_copy(
            src_ref=part.at[pl.ds(g * out_rows + start + k * piece, piece)],
            dst_ref=recv.at[row, pl.ds(start // n_col, piece)],
            send_sem=send1.at[index, g * n_col + k],
            recv_sem=recv1.at[index, row],
            device_id={"row": col * group + g, "col": k},
            device_id_type=MESH,
        )

    def scatter(index, wait):
        start, rows = spans[index]
        piece = rows // n_col
        for g in range(group):
            for k in range(n_col):
                mine = (col * group + g == row) & (col == k)

                @pl.when(jnp.logical_not(mine))
                def _(g=g, k=k):
                    copy = scatter_copy(index, g, k)
                    if wait:
                        copy.wait_send()
                    else:
                        copy.start()

                if not wait:
                    @pl.when(mine)
                    def _(g=g, k=k):
                        recv[row, pl.ds(start // n_col, piece)] = part[
                            pl.ds(g * out_rows + start + k * piece, piece)
                        ]

    def gather_copy(index, step):
        start, rows = spans[index]
        piece = rows // n_col
        here = out_ref.at[pl.ds(pl.multiple_of(start + col * piece, 8), piece)]
        return pltpu.make_async_remote_copy(
            src_ref=here,
            dst_ref=here,
            send_sem=send2.at[index, step],
            recv_sem=recv2.at[index, step],
            device_id={"row": row, "col": lax.rem(col + step, n_col)},
            device_id_type=MESH,
        )

    def reduce(index):
        start, rows = spans[index]
        piece = rows // n_col
        slot = pl.ds(start // n_col, piece)
        total = None
        for other in range(n_row):
            @pl.when(jnp.logical_not(home & (row == other)))
            def _(other=other):
                pltpu.make_async_remote_copy(
                    src_ref=part.at[pl.ds(start, piece)],
                    dst_ref=recv.at[other, slot],
                    send_sem=send1.at[index, 0],
                    recv_sem=recv1.at[index, other],
                    device_id={"row": other, "col": lax.div(row, group)},
                    device_id_type=MESH,
                ).wait_recv()

        for other in range(n_row):
            term = recv[other, slot]
            total = term if total is None else total + term
        out_ref[pl.ds(pl.multiple_of(start + col * piece, 8), piece)] = total
        for step in range(1, n_col):
            gather_copy(index, step).start()

    for index, (start, rows) in enumerate(compute):
        here = pl.ds(start, rows)

        def multiply(t, _, index=index, here=here):
            deep = pl.ds(pl.multiple_of(t * tile, tile), tile)
            load_a(index, t).wait()
            if index == 0:
                load_b(t).wait()
                high, low = split(b_ref[deep])
                if len(compute) > 1:
                    b_high[deep] = high
                    b_low[deep] = low
            else:
                high, low = b_high[deep], b_low[deep]
            part[here] += product(a_ref[here, deep], high, low)
            return 0

        part[here] = jnp.zeros_like(part[here])
        lax.fori_loop(0, tiles, multiply, 0)
        if index == 0:
            pl.semaphore_wait(barrier, n_row + n_col - 1 - home.astype(jnp.int32))
        scatter(index, False)
        if index > 0:
            reduce(index - 1)
    reduce(len(spans) - 1)
    for index, (start, rows) in enumerate(spans):
        piece = rows // n_col
        for step in range(1, n_col):
            owner = lax.rem(col + n_col - step, n_col)
            there = out_ref.at[pl.ds(pl.multiple_of(start + owner * piece, 8), piece)]
            pltpu.make_async_remote_copy(
                src_ref=there,
                dst_ref=there,
                send_sem=send2.at[index, step],
                recv_sem=recv2.at[index, step],
                device_id={"row": row, "col": owner},
                device_id_type=MESH,
            ).wait_recv()
    for index in range(len(spans)):
        scatter(index, True)
        for step in range(1, n_col):
            gather_copy(index, step).wait_send()


def shards(operator, basis):
    n_row = lax.axis_size("row")
    n_col = lax.axis_size("col")
    tile_rows, depth = operator.shape
    columns = basis.shape[1]
    group = n_row // n_col
    out_rows = tile_rows * n_col // n_row
    chunks = CHUNKS if group == 1 and sum(CHUNKS) == out_rows else (out_rows,)
    parts = len(chunks)
    tile = min(TILE, depth)
    tiles = depth // tile
    dma = pltpu.SemaphoreType.DMA
    split_shape = (depth, columns) if parts > 1 else (16, columns)
    return pl.pallas_call(
        functools.partial(kernel, n_row, n_col, chunks, tile),
        out_shape=jax.ShapeDtypeStruct((out_rows, columns), jnp.float32),
        in_specs=[pl.BlockSpec(memory_space=pl.ANY)] * 2,
        out_specs=pl.BlockSpec(memory_space=pltpu.VMEM),
        scratch_shapes=[
            pltpu.VMEM((tile_rows, depth), jnp.float32),
            pltpu.VMEM((depth, columns), jnp.float32),
            pltpu.VMEM(split_shape, jnp.bfloat16),
            pltpu.VMEM(split_shape, jnp.bfloat16),
            pltpu.VMEM((tile_rows, columns), jnp.float32),
            pltpu.VMEM((n_row, out_rows // n_col, columns), jnp.float32),
            dma((parts, tiles)),
            dma((tiles,)),
            dma((parts, n_row)),
            dma((parts, n_row)),
            dma((parts, n_col)),
            dma((parts, n_col)),
        ],
        compiler_params=pltpu.CompilerParams(
            collective_id=0, has_side_effects=True, vmem_limit_bytes=58 * 2**20
        ),
        cost_estimate=pl.CostEstimate(
            flops=6 * tile_rows * depth * columns,
            bytes_accessed=4 * (tile_rows * depth + depth * columns + out_rows * columns),
            transcendentals=0,
        ),
    )(operator, basis)


def solution(mesh):
    in_specs = (P(("reach", "col"), "row"), P(("reach", "row"), None))
    out_specs = P(("reach", "row"), None)
    return jax.shard_map(shards, mesh=mesh, in_specs=in_specs, out_specs=out_specs, check_vma=False)
```

```python
import functools

import jax
import jax.numpy as jnp
from jax import lax
from jax.experimental import pallas as pl
from jax.experimental.pallas import tpu as pltpu
from jax.sharding import PartitionSpec as P

MESH = pl.DeviceIdType.MESH
COMPUTE = 2
SPANS = 4
TILE = 2048


def split(values):
    high = values.astype(jnp.bfloat16)
    low = (values - high.astype(jnp.float32)).astype(jnp.bfloat16)
    return high, low


def product(a, b_high, b_low):
    rows = a.shape[0]
    high, low = split(a)
    both = jnp.dot(
        jnp.concatenate([high, low], axis=0), b_high, preferred_element_type=jnp.float32
    )
    cross = jnp.dot(high, b_low, preferred_element_type=jnp.float32)
    return both[:rows] + (both[rows:] + cross)


def kernel(
    n_row, n_col, steps, parts, tile,
    a_hbm, b_hbm, out_ref,
    a_ref, b_ref, b_high, b_low, part, recv,
    a_sem, b_sem, send1, recv1, send2, recv2,
):
    tile_rows, depth = a_hbm.shape
    tiles = depth // tile
    group = n_row // n_col
    out_rows = out_ref.shape[0]
    row, col = lax.axis_index("row"), lax.axis_index("col")
    home = lax.div(row, group) == col
    step_rows, span_rows = tile_rows // steps, out_rows // parts
    compute = [(index * step_rows, step_rows) for index in range(steps)]
    spans = [(index * span_rows, span_rows) for index in range(parts)]
    ratio = parts // steps

    def load_a(index, t):
        start, rows = compute[index]
        here = (pl.ds(start, rows), pl.ds(pl.multiple_of(t * tile, tile), tile))
        return pltpu.make_async_copy(a_hbm.at[here], a_ref.at[here], a_sem.at[index, t])

    def load_b(t):
        here = pl.ds(pl.multiple_of(t * tile, tile), tile)
        return pltpu.make_async_copy(b_hbm.at[here], b_ref.at[here], b_sem.at[t])

    def first_loads(t, _):
        load_b(t).start()
        load_a(0, t).start()
        return 0

    lax.fori_loop(0, tiles, first_loads, 0)

    for index in range(1, len(compute)):
        def later_loads(t, _, index=index):
            load_a(index, t).start()
            return 0

        lax.fori_loop(0, tiles, later_loads, 0)

    barrier = pltpu.get_barrier_semaphore()
    for other in range(n_row):
        @pl.when(jnp.logical_not(home & (row == other)))
        def _(other=other):
            pl.semaphore_signal(
                barrier, inc=1, device_id={"row": other, "col": lax.div(row, group)},
                device_id_type=MESH,
            )
    for step in range(1, n_col):
        pl.semaphore_signal(
            barrier, inc=1, device_id={"row": row, "col": lax.rem(col + step, n_col)},
            device_id_type=MESH,
        )

    def scatter_copy(index, g, k):
        start, rows = spans[index]
        piece = rows // n_col
        return pltpu.make_async_remote_copy(
            src_ref=part.at[pl.ds(g * out_rows + start + k * piece, piece)],
            dst_ref=recv.at[row, pl.ds(start // n_col, piece)],
            send_sem=send1.at[index, g * n_col + k],
            recv_sem=recv1.at[index, row],
            device_id={"row": col * group + g, "col": k},
            device_id_type=MESH,
        )

    def scatter(index, wait):
        start, rows = spans[index]
        piece = rows // n_col
        for g in range(group):
            for k in range(n_col):
                mine = (col * group + g == row) & (col == k)

                @pl.when(jnp.logical_not(mine))
                def _(g=g, k=k):
                    copy = scatter_copy(index, g, k)
                    if wait:
                        copy.wait_send()
                    else:
                        copy.start()

                if not wait:
                    @pl.when(mine)
                    def _(g=g, k=k):
                        recv[row, pl.ds(start // n_col, piece)] = part[
                            pl.ds(g * out_rows + start + k * piece, piece)
                        ]

    def gather_copy(index, step):
        start, rows = spans[index]
        piece = rows // n_col
        here = out_ref.at[pl.ds(pl.multiple_of(start + col * piece, 8), piece)]
        return pltpu.make_async_remote_copy(
            src_ref=here,
            dst_ref=here,
            send_sem=send2.at[index, step],
            recv_sem=recv2.at[index, step],
            device_id={"row": row, "col": lax.rem(col + step, n_col)},
            device_id_type=MESH,
        )

    def reduce(index):
        start, rows = spans[index]
        piece = rows // n_col
        slot = pl.ds(start // n_col, piece)
        total = None
        for other in range(n_row):
            @pl.when(jnp.logical_not(home & (row == other)))
            def _(other=other):
                pltpu.make_async_remote_copy(
                    src_ref=part.at[pl.ds(start, piece)],
                    dst_ref=recv.at[other, slot],
                    send_sem=send1.at[index, 0],
                    recv_sem=recv1.at[index, other],
                    device_id={"row": other, "col": lax.div(row, group)},
                    device_id_type=MESH,
                ).wait_recv()

        for other in range(n_row):
            term = recv[other, slot]
            total = term if total is None else total + term
        out_ref[pl.ds(pl.multiple_of(start + col * piece, 8), piece)] = total
        for step in range(1, n_col):
            gather_copy(index, step).start()

    for index, (start, rows) in enumerate(compute):
        here = pl.ds(start, rows)

        def multiply(t, _, index=index, here=here):
            deep = pl.ds(pl.multiple_of(t * tile, tile), tile)
            load_a(index, t).wait()
            if index == 0:
                load_b(t).wait()
                high, low = split(b_ref[deep])
                if steps > 1:
                    b_high[deep] = high
                    b_low[deep] = low
            else:
                high, low = b_high[deep], b_low[deep]
            part[here] += product(a_ref[here, deep], high, low)
            return 0

        part[here] = jnp.zeros_like(part[here])
        if index == 0:
            lax.fori_loop(0, tiles, multiply, 0)
            pl.semaphore_wait(barrier, n_row + n_col - 1 - home.astype(jnp.int32))
        else:
            middle = tiles * 3 // 4
            lax.fori_loop(0, middle, multiply, 0)
            for span in range((index - 1) * ratio, index * ratio):
                reduce(span)
            lax.fori_loop(middle, tiles, multiply, 0)
        for span in range(index * ratio, (index + 1) * ratio):
            scatter(span, False)
    for span in range((steps - 1) * ratio, parts):
        reduce(span)
    for index, (start, rows) in enumerate(spans):
        piece = rows // n_col
        for step in range(1, n_col):
            owner = lax.rem(col + n_col - step, n_col)
            there = out_ref.at[pl.ds(pl.multiple_of(start + owner * piece, 8), piece)]
            pltpu.make_async_remote_copy(
                src_ref=there,
                dst_ref=there,
                send_sem=send2.at[index, step],
                recv_sem=recv2.at[index, step],
                device_id={"row": row, "col": owner},
                device_id_type=MESH,
            ).wait_recv()
    for index in range(len(spans)):
        scatter(index, True)
        for step in range(1, n_col):
            gather_copy(index, step).wait_send()


def shards(operator, basis):
    n_row = lax.axis_size("row")
    n_col = lax.axis_size("col")
    tile_rows, depth = operator.shape
    columns = basis.shape[1]
    group = n_row // n_col
    out_rows = tile_rows * n_col // n_row
    steps, parts = (COMPUTE, SPANS) if group == 1 else (1, 1)
    tile = min(TILE, depth)
    tiles = depth // tile
    dma = pltpu.SemaphoreType.DMA
    split_shape = (depth, columns) if steps > 1 else (16, columns)
    return pl.pallas_call(
        functools.partial(kernel, n_row, n_col, steps, parts, tile),
        out_shape=jax.ShapeDtypeStruct((out_rows, columns), jnp.float32),
        in_specs=[pl.BlockSpec(memory_space=pl.ANY)] * 2,
        out_specs=pl.BlockSpec(memory_space=pltpu.VMEM),
        scratch_shapes=[
            pltpu.VMEM((tile_rows, depth), jnp.float32),
            pltpu.VMEM((depth, columns), jnp.float32),
            pltpu.VMEM(split_shape, jnp.bfloat16),
            pltpu.VMEM(split_shape, jnp.bfloat16),
            pltpu.VMEM((tile_rows, columns), jnp.float32),
            pltpu.VMEM((n_row, out_rows // n_col, columns), jnp.float32),
            dma((steps, tiles)),
            dma((tiles,)),
            dma((parts, n_row)),
            dma((parts, n_row)),
            dma((parts, n_col)),
            dma((parts, n_col)),
        ],
        compiler_params=pltpu.CompilerParams(
            collective_id=0, has_side_effects=True, vmem_limit_bytes=58 * 2**20
        ),
        cost_estimate=pl.CostEstimate(
            flops=6 * tile_rows * depth * columns,
            bytes_accessed=4 * (tile_rows * depth + depth * columns + out_rows * columns),
            transcendentals=0,
        ),
    )(operator, basis)


def solution(mesh):
    in_specs = (P(("reach", "col"), "row"), P(("reach", "row"), None))
    out_specs = P(("reach", "row"), None)
    return jax.shard_map(shards, mesh=mesh, in_specs=in_specs, out_specs=out_specs, check_vma=False)
```

```python
import functools

import jax
import jax.numpy as jnp
from jax import lax
from jax.experimental import pallas as pl
from jax.experimental.pallas import tpu as pltpu
from jax.sharding import PartitionSpec as P

MESH = pl.DeviceIdType.MESH
COMPUTE = 2
SPANS = 4
TILE = 2048


def split(values):
    high = values.astype(jnp.bfloat16)
    low = (values - high.astype(jnp.float32)).astype(jnp.bfloat16)
    return high, low


def product(a_split, high, low):
    rows = a_split.shape[0] // 2
    both = jnp.dot(a_split[...], high, preferred_element_type=jnp.float32)
    cross = jnp.dot(a_split[:rows], low, preferred_element_type=jnp.float32)
    return both[:rows] + (both[rows:] + cross)


def kernel(
    n_row, n_col, steps, parts, tile,
    a_hbm, b_hbm, out_ref,
    a_ref, b_ref, a_even, a_odd, high_even, high_odd, low_even, low_odd, part, recv,
    a_sem, b_sem, send1, recv1, send2, recv2,
):
    tile_rows, depth = a_hbm.shape
    tiles = depth // tile
    group = n_row // n_col
    out_rows = out_ref.shape[0]
    row, col = lax.axis_index("row"), lax.axis_index("col")
    home = lax.div(row, group) == col
    step_rows, span_rows = tile_rows // steps, out_rows // parts
    compute = [(index * step_rows, step_rows) for index in range(steps)]
    spans = [(index * span_rows, span_rows) for index in range(parts)]
    ratio = parts // steps

    def load_a(index, t):
        start, rows = compute[index]
        here = (pl.ds(start, rows), pl.ds(pl.multiple_of(t * tile, tile), tile))
        return pltpu.make_async_copy(a_hbm.at[here], a_ref.at[here], a_sem.at[index, t])

    def load_b(t):
        here = pl.ds(pl.multiple_of(t * tile, tile), tile)
        return pltpu.make_async_copy(b_hbm.at[here], b_ref.at[here], b_sem.at[t])

    def first_loads(t, _):
        load_b(t).start()
        load_a(0, t).start()
        return 0

    lax.fori_loop(0, tiles, first_loads, 0)

    for index in range(1, len(compute)):
        def later_loads(t, _, index=index):
            load_a(index, t).start()
            return 0

        lax.fori_loop(0, tiles, later_loads, 0)

    barrier = pltpu.get_barrier_semaphore()
    for other in range(n_row):
        @pl.when(jnp.logical_not(home & (row == other)))
        def _(other=other):
            pl.semaphore_signal(
                barrier, inc=1, device_id={"row": other, "col": lax.div(row, group)},
                device_id_type=MESH,
            )
    for step in range(1, n_col):
        pl.semaphore_signal(
            barrier, inc=1, device_id={"row": row, "col": lax.rem(col + step, n_col)},
            device_id_type=MESH,
        )

    def scatter_copy(index, g, k):
        start, rows = spans[index]
        piece = rows // n_col
        return pltpu.make_async_remote_copy(
            src_ref=part.at[pl.ds(g * out_rows + start + k * piece, piece)],
            dst_ref=recv.at[row, pl.ds(start // n_col, piece)],
            send_sem=send1.at[index, g * n_col + k],
            recv_sem=recv1.at[index, row],
            device_id={"row": col * group + g, "col": k},
            device_id_type=MESH,
        )

    def scatter(index, wait):
        start, rows = spans[index]
        piece = rows // n_col
        for g in range(group):
            for k in range(n_col):
                mine = (col * group + g == row) & (col == k)

                @pl.when(jnp.logical_not(mine))
                def _(g=g, k=k):
                    copy = scatter_copy(index, g, k)
                    if wait:
                        copy.wait_send()
                    else:
                        copy.start()

                if not wait:
                    @pl.when(mine)
                    def _(g=g, k=k):
                        recv[row, pl.ds(start // n_col, piece)] = part[
                            pl.ds(g * out_rows + start + k * piece, piece)
                        ]

    def gather_copy(index, step):
        start, rows = spans[index]
        piece = rows // n_col
        here = out_ref.at[pl.ds(pl.multiple_of(start + col * piece, 8), piece)]
        return pltpu.make_async_remote_copy(
            src_ref=here,
            dst_ref=here,
            send_sem=send2.at[index, step],
            recv_sem=recv2.at[index, step],
            device_id={"row": row, "col": lax.rem(col + step, n_col)},
            device_id_type=MESH,
        )

    def reduce(index):
        start, rows = spans[index]
        piece = rows // n_col
        slot = pl.ds(start // n_col, piece)
        total = None
        for other in range(n_row):
            @pl.when(jnp.logical_not(home & (row == other)))
            def _(other=other):
                pltpu.make_async_remote_copy(
                    src_ref=part.at[pl.ds(start, piece)],
                    dst_ref=recv.at[other, slot],
                    send_sem=send1.at[index, 0],
                    recv_sem=recv1.at[index, other],
                    device_id={"row": other, "col": lax.div(row, group)},
                    device_id_type=MESH,
                ).wait_recv()

        for other in range(n_row):
            term = recv[other, slot]
            total = term if total is None else total + term
        out_ref[pl.ds(pl.multiple_of(start + col * piece, 8), piece)] = total
        for step in range(1, n_col):
            gather_copy(index, step).start()

    a_split = (a_even, a_odd)
    b_high, b_low = (high_even, high_odd), (low_even, low_odd)

    def prepare(index, t, parity):
        start, rows = compute[index]
        deep = pl.ds(pl.multiple_of(t * tile, tile), tile)
        high, low = split(a_ref[pl.ds(start, rows), deep])
        a_split[parity][:rows] = high
        a_split[parity][rows:] = low
        if index == 0:
            kept = pl.ds(pl.multiple_of(lax.div(t, 2) * tile, tile), tile)
            high, low = split(b_ref[deep])
            b_high[parity][kept] = high
            b_low[parity][kept] = low

    def arrive(index, t):
        load_a(index, t).wait()
        if index == 0:
            load_b(t).wait()

    def multiply(index, t, parity):
        here = pl.ds(*compute[index])
        kept = pl.ds(pl.multiple_of(lax.div(t, 2) * tile, tile), tile)
        part[here] += product(a_split[parity], b_high[parity][kept], b_low[parity][kept])

    def pair(index, t, following):
        arrive(index, t + 1)
        if following is not None:
            arrive(*following)
        prepare(index, t + 1, 1)
        multiply(index, t, 0)
        if following is not None:
            prepare(*following, 0)
        multiply(index, t + 1, 1)

    def pairs(index, begin, end):
        def body(p, _):
            pair(index, 2 * p, (index, 2 * p + 2))
            return 0

        lax.fori_loop(begin, end, body, 0)

    part[...] = jnp.zeros_like(part)
    arrive(0, 0)
    prepare(0, 0, 0)
    for index in range(steps):
        pairs(index, 0, tiles // 2 - 1)
        if index > 0:
            for span in range((index - 1) * ratio, index * ratio):
                reduce(span)
        pair(index, tiles - 2, (index + 1, 0) if index + 1 < steps else None)
        if index == 0:
            pl.semaphore_wait(barrier, n_row + n_col - 1 - home.astype(jnp.int32))
        for span in range(index * ratio, (index + 1) * ratio):
            scatter(span, False)
    for span in range((steps - 1) * ratio, parts):
        reduce(span)
    for index, (start, rows) in enumerate(spans):
        piece = rows // n_col
        for step in range(1, n_col):
            owner = lax.rem(col + n_col - step, n_col)
            there = out_ref.at[pl.ds(pl.multiple_of(start + owner * piece, 8), piece)]
            pltpu.make_async_remote_copy(
                src_ref=there,
                dst_ref=there,
                send_sem=send2.at[index, step],
                recv_sem=recv2.at[index, step],
                device_id={"row": row, "col": owner},
                device_id_type=MESH,
            ).wait_recv()
    for index in range(len(spans)):
        scatter(index, True)
        for step in range(1, n_col):
            gather_copy(index, step).wait_send()


def shards(operator, basis):
    n_row = lax.axis_size("row")
    n_col = lax.axis_size("col")
    tile_rows, depth = operator.shape
    columns = basis.shape[1]
    group = n_row // n_col
    out_rows = tile_rows * n_col // n_row
    steps, parts = (COMPUTE, SPANS) if group == 1 else (1, 1)
    tile = min(TILE, depth // 2)
    tiles = depth // tile
    dma = pltpu.SemaphoreType.DMA
    a_split = pltpu.VMEM((2 * tile_rows // steps, tile), jnp.bfloat16)
    b_split = pltpu.VMEM((depth // 2, columns), jnp.bfloat16)
    return pl.pallas_call(
        functools.partial(kernel, n_row, n_col, steps, parts, tile),
        out_shape=jax.ShapeDtypeStruct((out_rows, columns), jnp.float32),
        in_specs=[pl.BlockSpec(memory_space=pl.ANY)] * 2,
        out_specs=pl.BlockSpec(memory_space=pltpu.VMEM),
        scratch_shapes=[
            pltpu.VMEM((tile_rows, depth), jnp.float32),
            pltpu.VMEM((depth, columns), jnp.float32),
            a_split,
            a_split,
            b_split,
            b_split,
            b_split,
            b_split,
            pltpu.VMEM((tile_rows, columns), jnp.float32),
            pltpu.VMEM((n_row, out_rows // n_col, columns), jnp.float32),
            dma((steps, tiles)),
            dma((tiles,)),
            dma((parts, n_row)),
            dma((parts, n_row)),
            dma((parts, n_col)),
            dma((parts, n_col)),
        ],
        compiler_params=pltpu.CompilerParams(
            collective_id=0, has_side_effects=True, vmem_limit_bytes=58 * 2**20
        ),
        cost_estimate=pl.CostEstimate(
            flops=6 * tile_rows * depth * columns,
            bytes_accessed=4 * (tile_rows * depth + depth * columns + out_rows * columns),
            transcendentals=0,
        ),
    )(operator, basis)


def solution(mesh):
    in_specs = (P(("reach", "col"), "row"), P(("reach", "row"), None))
    out_specs = P(("reach", "row"), None)
    return jax.shard_map(shards, mesh=mesh, in_specs=in_specs, out_specs=out_specs, check_vma=False)
```

```python
import functools

import jax
import jax.numpy as jnp
from jax import lax
from jax.experimental import pallas as pl
from jax.experimental.pallas import tpu as pltpu
from jax.sharding import PartitionSpec as P

MESH = pl.DeviceIdType.MESH
COMPUTE = 2
SPANS = 4
TILE = 2048


def split(values):
    high = values.astype(jnp.bfloat16)
    low = (values - high.astype(jnp.float32)).astype(jnp.bfloat16)
    return high, low


def product(a, b_high, b_low):
    rows = a.shape[0]
    high, low = split(a)
    both = jnp.dot(
        jnp.concatenate([high, low], axis=0), b_high, preferred_element_type=jnp.float32
    )
    cross = jnp.dot(high, b_low, preferred_element_type=jnp.float32)
    return both[:rows] + (both[rows:] + cross)


def kernel(
    n_row, n_col, steps, parts, tile,
    a_hbm, b_hbm, out_ref,
    a_ref, b_ref, b_high, b_low, part, mid, recv,
    a_sem, b_sem, send1, recv1, send2, recv2, send3, recv3,
):
    tile_rows, depth = a_hbm.shape
    tiles = depth // tile
    group = n_row // n_col
    out_rows = out_ref.shape[0]
    row, col = lax.axis_index("row"), lax.axis_index("col")
    step_rows, span_rows = tile_rows // steps, out_rows // parts
    compute = [(index * step_rows, step_rows) for index in range(steps)]
    spans = [(index * span_rows, span_rows) for index in range(parts)]
    ratio = parts // steps

    def load_a(index, t):
        start, rows = compute[index]
        here = (pl.ds(start, rows), pl.ds(pl.multiple_of(t * tile, tile), tile))
        return pltpu.make_async_copy(a_hbm.at[here], a_ref.at[here], a_sem.at[index, t])

    def load_b(t):
        here = pl.ds(pl.multiple_of(t * tile, tile), tile)
        return pltpu.make_async_copy(b_hbm.at[here], b_ref.at[here], b_sem.at[t])

    def first_loads(t, _):
        load_b(t).start()
        load_a(0, t).start()
        return 0

    lax.fori_loop(0, tiles, first_loads, 0)

    for index in range(1, len(compute)):
        def later_loads(t, _, index=index):
            load_a(index, t).start()
            return 0

        lax.fori_loop(0, tiles, later_loads, 0)

    barrier = pltpu.get_barrier_semaphore()
    for step in range(1, n_col):
        pl.semaphore_signal(
            barrier, inc=1, device_id={"row": row, "col": lax.rem(col + step, n_col)},
            device_id_type=MESH,
        )
    for step in range(1, n_row):
        pl.semaphore_signal(
            barrier, inc=1, device_id={"row": lax.rem(row + step, n_row), "col": col},
            device_id_type=MESH,
        )

    def piece_of(index):
        start, rows = spans[index]
        return start, rows // n_col, pl.ds(start // n_col, rows // n_col)

    def stage1(index, step, g):
        start, piece, slot = piece_of(index)
        other = lax.rem(col + step, n_col)
        first = pl.multiple_of(g * out_rows + start + other * piece, 8)
        return pltpu.make_async_remote_copy(
            src_ref=part.at[pl.ds(first, piece)],
            dst_ref=mid.at[col * group + g, slot],
            send_sem=send1.at[index, step * group + g],
            recv_sem=recv1.at[index, step * group + g],
            device_id={"row": row, "col": other},
            device_id_type=MESH,
        )

    def arrive1(index, step, g):
        start, piece, slot = piece_of(index)
        other = lax.rem(col + n_col - step, n_col)
        pltpu.make_async_remote_copy(
            src_ref=part.at[pl.ds(start, piece)],
            dst_ref=mid.at[other * group + g, slot],
            send_sem=send1.at[index, step * group + g],
            recv_sem=recv1.at[index, step * group + g],
            device_id={"row": row, "col": other},
            device_id_type=MESH,
        ).wait_recv()

    def stage2(index, step):
        slot = piece_of(index)[2]
        other = lax.rem(row + step, n_row)
        return pltpu.make_async_remote_copy(
            src_ref=mid.at[other, slot],
            dst_ref=recv.at[step, slot],
            send_sem=send2.at[index, step],
            recv_sem=recv2.at[index, step],
            device_id={"row": other, "col": col},
            device_id_type=MESH,
        )

    def stage3(index, step):
        start, piece, _ = piece_of(index)
        here = out_ref.at[pl.ds(pl.multiple_of(start + col * piece, 8), piece)]
        return pltpu.make_async_remote_copy(
            src_ref=here,
            dst_ref=here,
            send_sem=send3.at[index, step],
            recv_sem=recv3.at[index, step],
            device_id={"row": row, "col": lax.rem(col + step, n_col)},
            device_id_type=MESH,
        )

    def arrive3(index, step):
        start, piece, _ = piece_of(index)
        other = lax.rem(col + n_col - step, n_col)
        there = out_ref.at[pl.ds(pl.multiple_of(start + other * piece, 8), piece)]
        pltpu.make_async_remote_copy(
            src_ref=there,
            dst_ref=there,
            send_sem=send3.at[index, step],
            recv_sem=recv3.at[index, step],
            device_id={"row": row, "col": other},
            device_id_type=MESH,
        ).wait_recv()

    def scatter(index):
        start, piece, slot = piece_of(index)
        for step in range(1, n_col):
            for g in range(group):
                stage1(index, step, g).start()
        for g in range(group):
            first = pl.multiple_of(g * out_rows + start + col * piece, 8)
            mid[col * group + g, slot] = part[pl.ds(first, piece)]

    def forward(index):
        for step in range(1, n_col):
            for g in range(group):
                arrive1(index, step, g)
        for step in range(1, n_row):
            stage2(index, step).start()

    def reduce(index):
        start, piece, slot = piece_of(index)
        total = mid[row, slot]
        for step in range(1, n_row):
            stage2(index, step).wait_recv()
            total = total + recv[step, slot]
        out_ref[pl.ds(pl.multiple_of(start + col * piece, 8), piece)] = total
        for step in range(1, n_col):
            stage3(index, step).start()

    for index, (start, rows) in enumerate(compute):
        here = pl.ds(start, rows)

        def multiply(t, _, index=index, here=here):
            deep = pl.ds(pl.multiple_of(t * tile, tile), tile)
            load_a(index, t).wait()
            if index == 0:
                load_b(t).wait()
                high, low = split(b_ref[deep])
                if steps > 1:
                    b_high[deep] = high
                    b_low[deep] = low
            else:
                high, low = b_high[deep], b_low[deep]
            part[here] += product(a_ref[here, deep], high, low)
            return 0

        part[here] = jnp.zeros_like(part[here])
        middle = tiles // 2 if index > 0 else 0
        lax.fori_loop(0, middle, multiply, 0)
        if index > 0:
            for span in range((index - 1) * ratio, index * ratio):
                forward(span)
        lax.fori_loop(middle, tiles, multiply, 0)
        if index == 0:
            pl.semaphore_wait(barrier, n_row + n_col - 2)
        for span in range(index * ratio, (index + 1) * ratio):
            scatter(span)
        if index > 0:
            for span in range((index - 1) * ratio, index * ratio):
                reduce(span)
    for span in range((steps - 1) * ratio, parts):
        forward(span)
    for span in range((steps - 1) * ratio, parts):
        reduce(span)
    for span in range(parts):
        for step in range(1, n_col):
            arrive3(span, step)
    for span in range(parts):
        for step in range(1, n_col):
            for g in range(group):
                stage1(span, step, g).wait_send()
            stage3(span, step).wait_send()
        for step in range(1, n_row):
            stage2(span, step).wait_send()


def shards(operator, basis):
    n_row = lax.axis_size("row")
    n_col = lax.axis_size("col")
    tile_rows, depth = operator.shape
    columns = basis.shape[1]
    group = n_row // n_col
    out_rows = tile_rows * n_col // n_row
    steps, parts = (COMPUTE, SPANS) if group == 1 else (1, 1)
    tile = min(TILE, depth)
    tiles = depth // tile
    dma = pltpu.SemaphoreType.DMA
    split_shape = (depth, columns) if steps > 1 else (16, columns)
    return pl.pallas_call(
        functools.partial(kernel, n_row, n_col, steps, parts, tile),
        out_shape=jax.ShapeDtypeStruct((out_rows, columns), jnp.float32),
        in_specs=[pl.BlockSpec(memory_space=pl.ANY)] * 2,
        out_specs=pl.BlockSpec(memory_space=pltpu.VMEM),
        scratch_shapes=[
            pltpu.VMEM((tile_rows, depth), jnp.float32),
            pltpu.VMEM((depth, columns), jnp.float32),
            pltpu.VMEM(split_shape, jnp.bfloat16),
            pltpu.VMEM(split_shape, jnp.bfloat16),
            pltpu.VMEM((tile_rows, columns), jnp.float32),
            pltpu.VMEM((n_row, out_rows // n_col, columns), jnp.float32),
            pltpu.VMEM((n_row, out_rows // n_col, columns), jnp.float32),
            dma((steps, tiles)),
            dma((tiles,)),
            dma((parts, n_row)),
            dma((parts, n_row)),
            dma((parts, n_row)),
            dma((parts, n_row)),
            dma((parts, n_col)),
            dma((parts, n_col)),
        ],
        compiler_params=pltpu.CompilerParams(
            collective_id=0, has_side_effects=True, vmem_limit_bytes=58 * 2**20
        ),
        cost_estimate=pl.CostEstimate(
            flops=6 * tile_rows * depth * columns,
            bytes_accessed=4 * (tile_rows * depth + depth * columns + out_rows * columns),
            transcendentals=0,
        ),
    )(operator, basis)


def solution(mesh):
    in_specs = (P(("reach", "col"), "row"), P(("reach", "row"), None))
    out_specs = P(("reach", "row"), None)
    return jax.shard_map(shards, mesh=mesh, in_specs=in_specs, out_specs=out_specs, check_vma=False)
```

```python
import functools

import jax
import jax.numpy as jnp
from jax import lax
from jax.experimental import pallas as pl
from jax.experimental.pallas import tpu as pltpu
from jax.sharding import PartitionSpec as P

MESH = pl.DeviceIdType.MESH
COMPUTE = 2
SPANS = 4
TILE = 2048


def split(values):
    high = values.astype(jnp.bfloat16)
    low = (values - high.astype(jnp.float32)).astype(jnp.bfloat16)
    return high, low


def product(a, b_high, b_low):
    high, low = split(a)
    dot = functools.partial(jnp.dot, preferred_element_type=jnp.float32)
    return dot(high, b_high) + (dot(low, b_high) + dot(high, b_low))


def kernel(
    n_row, n_col, steps, parts, tile,
    a_hbm, b_hbm, out_ref,
    a_ref, b_ref, b_high, b_low, part, mid, recv,
    a_sem, b_sem, send1, recv1, send2, recv2, send3, recv3,
):
    tile_rows, depth = a_hbm.shape
    tiles = depth // tile
    group = n_row // n_col
    out_rows = out_ref.shape[0]
    row, col = lax.axis_index("row"), lax.axis_index("col")
    step_rows, span_rows = tile_rows // steps, out_rows // parts
    compute = [(index * step_rows, step_rows) for index in range(steps)]
    spans = [(index * span_rows, span_rows) for index in range(parts)]
    ratio = parts // steps

    def load_a(index, t):
        start, rows = compute[index]
        here = (pl.ds(start, rows), pl.ds(pl.multiple_of(t * tile, tile), tile))
        return pltpu.make_async_copy(a_hbm.at[here], a_ref.at[here], a_sem.at[index, t])

    def load_b(t):
        here = pl.ds(pl.multiple_of(t * tile, tile), tile)
        return pltpu.make_async_copy(b_hbm.at[here], b_ref.at[here], b_sem.at[t])

    def first_loads(t, _):
        load_b(t).start()
        load_a(0, t).start()
        return 0

    lax.fori_loop(0, tiles, first_loads, 0)

    for index in range(1, len(compute)):
        def later_loads(t, _, index=index):
            load_a(index, t).start()
            return 0

        lax.fori_loop(0, tiles, later_loads, 0)

    barrier = pltpu.get_barrier_semaphore()
    for step in range(1, n_col):
        pl.semaphore_signal(
            barrier, inc=1, device_id={"row": row, "col": lax.rem(col + step, n_col)},
            device_id_type=MESH,
        )
    for step in range(1, n_row):
        pl.semaphore_signal(
            barrier, inc=1, device_id={"row": lax.rem(row + step, n_row), "col": col},
            device_id_type=MESH,
        )

    def piece_of(index):
        start, rows = spans[index]
        return start, rows // n_col, pl.ds(start // n_col, rows // n_col)

    def stage1(index, step, g):
        start, piece, slot = piece_of(index)
        other = lax.rem(col + step, n_col)
        first = pl.multiple_of(g * out_rows + start + other * piece, 8)
        return pltpu.make_async_remote_copy(
            src_ref=part.at[pl.ds(first, piece)],
            dst_ref=mid.at[col * group + g, slot],
            send_sem=send1.at[index, step * group + g],
            recv_sem=recv1.at[index, step * group + g],
            device_id={"row": row, "col": other},
            device_id_type=MESH,
        )

    def arrive1(index, step, g):
        start, piece, slot = piece_of(index)
        other = lax.rem(col + n_col - step, n_col)
        pltpu.make_async_remote_copy(
            src_ref=part.at[pl.ds(start, piece)],
            dst_ref=mid.at[other * group + g, slot],
            send_sem=send1.at[index, step * group + g],
            recv_sem=recv1.at[index, step * group + g],
            device_id={"row": row, "col": other},
            device_id_type=MESH,
        ).wait_recv()

    def stage2(index, step):
        slot = piece_of(index)[2]
        other = lax.rem(row + step, n_row)
        return pltpu.make_async_remote_copy(
            src_ref=mid.at[other, slot],
            dst_ref=recv.at[step, slot],
            send_sem=send2.at[index, step],
            recv_sem=recv2.at[index, step],
            device_id={"row": other, "col": col},
            device_id_type=MESH,
        )

    def stage3(index, step):
        start, piece, _ = piece_of(index)
        here = out_ref.at[pl.ds(pl.multiple_of(start + col * piece, 8), piece)]
        return pltpu.make_async_remote_copy(
            src_ref=here,
            dst_ref=here,
            send_sem=send3.at[index, step],
            recv_sem=recv3.at[index, step],
            device_id={"row": row, "col": lax.rem(col + step, n_col)},
            device_id_type=MESH,
        )

    def arrive3(index, step):
        start, piece, _ = piece_of(index)
        other = lax.rem(col + n_col - step, n_col)
        there = out_ref.at[pl.ds(pl.multiple_of(start + other * piece, 8), piece)]
        pltpu.make_async_remote_copy(
            src_ref=there,
            dst_ref=there,
            send_sem=send3.at[index, step],
            recv_sem=recv3.at[index, step],
            device_id={"row": row, "col": other},
            device_id_type=MESH,
        ).wait_recv()

    def scatter(index):
        start, piece, slot = piece_of(index)
        for step in range(1, n_col):
            for g in range(group):
                stage1(index, step, g).start()
        for g in range(group):
            first = pl.multiple_of(g * out_rows + start + col * piece, 8)
            mid[col * group + g, slot] = part[pl.ds(first, piece)]

    def forward(index):
        for step in range(1, n_col):
            for g in range(group):
                arrive1(index, step, g)
        for step in range(1, n_row):
            stage2(index, step).start()

    def reduce(index):
        start, piece, slot = piece_of(index)
        total = mid[row, slot]
        for step in range(1, n_row):
            stage2(index, step).wait_recv()
            total = total + recv[step, slot]
        out_ref[pl.ds(pl.multiple_of(start + col * piece, 8), piece)] = total
        for step in range(1, n_col):
            stage3(index, step).start()

    for index, (start, rows) in enumerate(compute):
        here = pl.ds(start, rows)

        def multiply(t, _, index=index, here=here):
            deep = pl.ds(pl.multiple_of(t * tile, tile), tile)
            load_a(index, t).wait()
            if index == 0:
                load_b(t).wait()
                high, low = split(b_ref[deep])
                if steps > 1:
                    b_high[deep] = high
                    b_low[deep] = low
            else:
                high, low = b_high[deep], b_low[deep]
            part[here] += product(a_ref[here, deep], high, low)
            return 0

        part[here] = jnp.zeros_like(part[here])
        middle = tiles // 2 if index > 0 else 0
        lax.fori_loop(0, middle, multiply, 0)
        if index > 0:
            for span in range((index - 1) * ratio, index * ratio):
                forward(span)
        lax.fori_loop(middle, tiles, multiply, 0)
        if index == 0:
            pl.semaphore_wait(barrier, n_row + n_col - 2)
        for span in range(index * ratio, (index + 1) * ratio):
            scatter(span)
        if index > 0:
            for span in range((index - 1) * ratio, index * ratio):
                reduce(span)
    for span in range((steps - 1) * ratio, parts):
        forward(span)
    for span in range((steps - 1) * ratio, parts):
        reduce(span)
    for span in range(parts):
        for step in range(1, n_col):
            arrive3(span, step)
    for span in range(parts):
        for step in range(1, n_col):
            for g in range(group):
                stage1(span, step, g).wait_send()
            stage3(span, step).wait_send()
        for step in range(1, n_row):
            stage2(span, step).wait_send()


def shards(operator, basis):
    n_row = lax.axis_size("row")
    n_col = lax.axis_size("col")
    tile_rows, depth = operator.shape
    columns = basis.shape[1]
    group = n_row // n_col
    out_rows = tile_rows * n_col // n_row
    steps, parts = (COMPUTE, SPANS) if group == 1 else (1, 1)
    tile = min(TILE, depth)
    tiles = depth // tile
    dma = pltpu.SemaphoreType.DMA
    split_shape = (depth, columns) if steps > 1 else (16, columns)
    return pl.pallas_call(
        functools.partial(kernel, n_row, n_col, steps, parts, tile),
        out_shape=jax.ShapeDtypeStruct((out_rows, columns), jnp.float32),
        in_specs=[pl.BlockSpec(memory_space=pl.ANY)] * 2,
        out_specs=pl.BlockSpec(memory_space=pltpu.VMEM),
        scratch_shapes=[
            pltpu.VMEM((tile_rows, depth), jnp.float32),
            pltpu.VMEM((depth, columns), jnp.float32),
            pltpu.VMEM(split_shape, jnp.bfloat16),
            pltpu.VMEM(split_shape, jnp.bfloat16),
            pltpu.VMEM((tile_rows, columns), jnp.float32),
            pltpu.VMEM((n_row, out_rows // n_col, columns), jnp.float32),
            pltpu.VMEM((n_row, out_rows // n_col, columns), jnp.float32),
            dma((steps, tiles)),
            dma((tiles,)),
            dma((parts, n_row)),
            dma((parts, n_row)),
            dma((parts, n_row)),
            dma((parts, n_row)),
            dma((parts, n_col)),
            dma((parts, n_col)),
        ],
        compiler_params=pltpu.CompilerParams(
            collective_id=0, has_side_effects=True, vmem_limit_bytes=58 * 2**20
        ),
        cost_estimate=pl.CostEstimate(
            flops=6 * tile_rows * depth * columns,
            bytes_accessed=4 * (tile_rows * depth + depth * columns + out_rows * columns),
            transcendentals=0,
        ),
    )(operator, basis)


def solution(mesh):
    in_specs = (P(("reach", "col"), "row"), P(("reach", "row"), None))
    out_specs = P(("reach", "row"), None)
    return jax.shard_map(shards, mesh=mesh, in_specs=in_specs, out_specs=out_specs, check_vma=False)
```

```python
import functools

import jax
import jax.numpy as jnp
from jax import lax
from jax.experimental import pallas as pl
from jax.experimental.pallas import tpu as pltpu
from jax.sharding import PartitionSpec as P

MESH = pl.DeviceIdType.MESH
COMPUTE = 2
SPANS = 4
TILE = 1024


def split(values):
    high = values.astype(jnp.bfloat16)
    low = (values - high.astype(jnp.float32)).astype(jnp.bfloat16)
    return high, low


def product(a, b_high, b_low):
    rows = a.shape[0]
    high, low = split(a)
    both = jnp.dot(
        jnp.concatenate([high, low], axis=0), b_high, preferred_element_type=jnp.float32
    )
    cross = jnp.dot(high, b_low, preferred_element_type=jnp.float32)
    return both[:rows] + (both[rows:] + cross)


def kernel(
    n_row, n_col, steps, parts, tile,
    a_hbm, b_hbm, out_ref,
    a_ref, b_ref, b_high, b_low, part, mid, recv,
    a_sem, b_sem, send1, recv1, send2, recv2, send3, recv3,
):
    tile_rows, depth = a_hbm.shape
    tiles = depth // tile
    group = n_row // n_col
    out_rows = out_ref.shape[0]
    row, col = lax.axis_index("row"), lax.axis_index("col")
    step_rows, span_rows = tile_rows // steps, out_rows // parts
    compute = [(index * step_rows, step_rows) for index in range(steps)]
    spans = [(index * span_rows, span_rows) for index in range(parts)]
    ratio = parts // steps

    def load_a(index, t):
        start, rows = compute[index]
        here = (pl.ds(start, rows), pl.ds(pl.multiple_of(t * tile, tile), tile))
        return pltpu.make_async_copy(a_hbm.at[here], a_ref.at[here], a_sem.at[index, t])

    def load_b(t):
        here = pl.ds(pl.multiple_of(t * tile, tile), tile)
        return pltpu.make_async_copy(b_hbm.at[here], b_ref.at[here], b_sem.at[t])

    def first_loads(t, _):
        load_b(t).start()
        load_a(0, t).start()
        return 0

    lax.fori_loop(0, tiles, first_loads, 0)

    for index in range(1, len(compute)):
        def later_loads(t, _, index=index):
            load_a(index, t).start()
            return 0

        lax.fori_loop(0, tiles, later_loads, 0)

    barrier = pltpu.get_barrier_semaphore()
    for step in range(1, n_col):
        pl.semaphore_signal(
            barrier, inc=1, device_id={"row": row, "col": lax.rem(col + step, n_col)},
            device_id_type=MESH,
        )
    for step in range(1, n_row):
        pl.semaphore_signal(
            barrier, inc=1, device_id={"row": lax.rem(row + step, n_row), "col": col},
            device_id_type=MESH,
        )

    def piece_of(index):
        start, rows = spans[index]
        return start, rows // n_col, pl.ds(start // n_col, rows // n_col)

    def stage1(index, step, g):
        start, piece, slot = piece_of(index)
        other = lax.rem(col + step, n_col)
        first = pl.multiple_of(g * out_rows + start + other * piece, 8)
        return pltpu.make_async_remote_copy(
            src_ref=part.at[pl.ds(first, piece)],
            dst_ref=mid.at[col * group + g, slot],
            send_sem=send1.at[index, step * group + g],
            recv_sem=recv1.at[index, step * group + g],
            device_id={"row": row, "col": other},
            device_id_type=MESH,
        )

    def arrive1(index, step, g):
        start, piece, slot = piece_of(index)
        other = lax.rem(col + n_col - step, n_col)
        pltpu.make_async_remote_copy(
            src_ref=part.at[pl.ds(start, piece)],
            dst_ref=mid.at[other * group + g, slot],
            send_sem=send1.at[index, step * group + g],
            recv_sem=recv1.at[index, step * group + g],
            device_id={"row": row, "col": other},
            device_id_type=MESH,
        ).wait_recv()

    def stage2(index, step):
        slot = piece_of(index)[2]
        other = lax.rem(row + step, n_row)
        return pltpu.make_async_remote_copy(
            src_ref=mid.at[other, slot],
            dst_ref=recv.at[step, slot],
            send_sem=send2.at[index, step],
            recv_sem=recv2.at[index, step],
            device_id={"row": other, "col": col},
            device_id_type=MESH,
        )

    def stage3(index, step):
        start, piece, _ = piece_of(index)
        here = out_ref.at[pl.ds(pl.multiple_of(start + col * piece, 8), piece)]
        return pltpu.make_async_remote_copy(
            src_ref=here,
            dst_ref=here,
            send_sem=send3.at[index, step],
            recv_sem=recv3.at[index, step],
            device_id={"row": row, "col": lax.rem(col + step, n_col)},
            device_id_type=MESH,
        )

    def arrive3(index, step):
        start, piece, _ = piece_of(index)
        other = lax.rem(col + n_col - step, n_col)
        there = out_ref.at[pl.ds(pl.multiple_of(start + other * piece, 8), piece)]
        pltpu.make_async_remote_copy(
            src_ref=there,
            dst_ref=there,
            send_sem=send3.at[index, step],
            recv_sem=recv3.at[index, step],
            device_id={"row": row, "col": other},
            device_id_type=MESH,
        ).wait_recv()

    def scatter(index):
        start, piece, slot = piece_of(index)
        for step in range(1, n_col):
            for g in range(group):
                stage1(index, step, g).start()
        for g in range(group):
            first = pl.multiple_of(g * out_rows + start + col * piece, 8)
            mid[col * group + g, slot] = part[pl.ds(first, piece)]

    def forward(index):
        for step in range(1, n_col):
            for g in range(group):
                arrive1(index, step, g)
        for step in range(1, n_row):
            stage2(index, step).start()

    def reduce(index):
        start, piece, slot = piece_of(index)
        total = mid[row, slot]
        for step in range(1, n_row):
            stage2(index, step).wait_recv()
            total = total + recv[step, slot]
        out_ref[pl.ds(pl.multiple_of(start + col * piece, 8), piece)] = total
        for step in range(1, n_col):
            stage3(index, step).start()

    for index, (start, rows) in enumerate(compute):
        here = pl.ds(start, rows)

        def multiply(t, _, index=index, here=here):
            deep = pl.ds(pl.multiple_of(t * tile, tile), tile)
            load_a(index, t).wait()
            if index == 0:
                load_b(t).wait()
                high, low = split(b_ref[deep])
                if steps > 1:
                    b_high[deep] = high
                    b_low[deep] = low
            else:
                high, low = b_high[deep], b_low[deep]
            part[here] += product(a_ref[here, deep], high, low)
            return 0

        part[here] = jnp.zeros_like(part[here])
        middle = tiles * 3 // 8 if index > 0 else 0
        lax.fori_loop(0, middle, multiply, 0)
        if index > 0:
            for span in range((index - 1) * ratio, index * ratio):
                forward(span)
        lax.fori_loop(middle, tiles, multiply, 0)
        if index == 0:
            pl.semaphore_wait(barrier, n_row + n_col - 2)
        for span in range(index * ratio, (index + 1) * ratio):
            scatter(span)
        if index > 0:
            for span in range((index - 1) * ratio, index * ratio):
                reduce(span)
    for span in range((steps - 1) * ratio, parts):
        forward(span)
    for span in range((steps - 1) * ratio, parts):
        reduce(span)
    for span in range(parts):
        for step in range(1, n_col):
            arrive3(span, step)
    for span in range(parts):
        for step in range(1, n_col):
            for g in range(group):
                stage1(span, step, g).wait_send()
            stage3(span, step).wait_send()
        for step in range(1, n_row):
            stage2(span, step).wait_send()


def shards(operator, basis):
    n_row = lax.axis_size("row")
    n_col = lax.axis_size("col")
    tile_rows, depth = operator.shape
    columns = basis.shape[1]
    group = n_row // n_col
    out_rows = tile_rows * n_col // n_row
    steps, parts = (COMPUTE, SPANS) if group == 1 else (1, 1)
    tile = min(TILE, depth)
    tiles = depth // tile
    dma = pltpu.SemaphoreType.DMA
    split_shape = (depth, columns) if steps > 1 else (16, columns)
    return pl.pallas_call(
        functools.partial(kernel, n_row, n_col, steps, parts, tile),
        out_shape=jax.ShapeDtypeStruct((out_rows, columns), jnp.float32),
        in_specs=[pl.BlockSpec(memory_space=pl.ANY)] * 2,
        out_specs=pl.BlockSpec(memory_space=pltpu.VMEM),
        scratch_shapes=[
            pltpu.VMEM((tile_rows, depth), jnp.float32),
            pltpu.VMEM((depth, columns), jnp.float32),
            pltpu.VMEM(split_shape, jnp.bfloat16),
            pltpu.VMEM(split_shape, jnp.bfloat16),
            pltpu.VMEM((tile_rows, columns), jnp.float32),
            pltpu.VMEM((n_row, out_rows // n_col, columns), jnp.float32),
            pltpu.VMEM((n_row, out_rows // n_col, columns), jnp.float32),
            dma((steps, tiles)),
            dma((tiles,)),
            dma((parts, n_row)),
            dma((parts, n_row)),
            dma((parts, n_row)),
            dma((parts, n_row)),
            dma((parts, n_col)),
            dma((parts, n_col)),
        ],
        compiler_params=pltpu.CompilerParams(
            collective_id=0, has_side_effects=True, vmem_limit_bytes=58 * 2**20
        ),
        cost_estimate=pl.CostEstimate(
            flops=6 * tile_rows * depth * columns,
            bytes_accessed=4 * (tile_rows * depth + depth * columns + out_rows * columns),
            transcendentals=0,
        ),
    )(operator, basis)


def solution(mesh):
    in_specs = (P(("reach", "col"), "row"), P(("reach", "row"), None))
    out_specs = P(("reach", "row"), None)
    return jax.shard_map(shards, mesh=mesh, in_specs=in_specs, out_specs=out_specs, check_vma=False)
```

```python
import functools

import jax
import jax.numpy as jnp
from jax import lax
from jax.experimental import pallas as pl
from jax.experimental.pallas import tpu as pltpu
from jax.sharding import PartitionSpec as P

MESH = pl.DeviceIdType.MESH
COMPUTE = 2
SPANS = 4
TILE = 2048


def split(values):
    high = values.astype(jnp.bfloat16)
    low = (values - high.astype(jnp.float32)).astype(jnp.bfloat16)
    return high, low


def product(a, b_high, b_low):
    rows = a.shape[0]
    high, low = split(a)
    both = jnp.dot(
        jnp.concatenate([high, low], axis=0), b_high, preferred_element_type=jnp.float32
    )
    cross = jnp.dot(high, b_low, preferred_element_type=jnp.float32)
    return both[:rows] + (both[rows:] + cross)


def kernel(
    n_row, n_col, steps, parts, tile,
    a_hbm, b_hbm, out_ref,
    a_ref, b_ref, b_high, b_low, part, mid, recv,
    a_sem, b_sem, send1, recv1, send2, recv2, send3, recv3,
):
    tile_rows, depth = a_hbm.shape
    tiles = depth // tile
    group = n_row // n_col
    out_rows = out_ref.shape[0]
    row, col = lax.axis_index("row"), lax.axis_index("col")
    step_rows, span_rows = tile_rows // steps, out_rows // parts
    compute = [(index * step_rows, step_rows) for index in range(steps)]
    spans = [(index * span_rows, span_rows) for index in range(parts)]
    ratio = parts // steps

    def deep_of(index):
        return tile if index == 0 else 2 * tile

    def load_a(index, t):
        start, rows = compute[index]
        deep = deep_of(index)
        here = (pl.ds(start, rows), pl.ds(pl.multiple_of(t * deep, deep), deep))
        return pltpu.make_async_copy(a_hbm.at[here], a_ref.at[here], a_sem.at[index, t])

    def load_b(t):
        here = pl.ds(pl.multiple_of(t * tile, tile), tile)
        return pltpu.make_async_copy(b_hbm.at[here], b_ref.at[here], b_sem.at[t])

    def first_loads(t, _):
        load_b(t).start()
        load_a(0, t).start()
        return 0

    lax.fori_loop(0, tiles, first_loads, 0)

    for index in range(1, len(compute)):
        def later_loads(t, _, index=index):
            load_a(index, t).start()
            return 0

        lax.fori_loop(0, tiles // 2, later_loads, 0)

    barrier = pltpu.get_barrier_semaphore()
    for step in range(1, n_col):
        pl.semaphore_signal(
            barrier, inc=1, device_id={"row": row, "col": lax.rem(col + step, n_col)},
            device_id_type=MESH,
        )
    for step in range(1, n_row):
        pl.semaphore_signal(
            barrier, inc=1, device_id={"row": lax.rem(row + step, n_row), "col": col},
            device_id_type=MESH,
        )

    def piece_of(index):
        start, rows = spans[index]
        return start, rows // n_col, pl.ds(start // n_col, rows // n_col)

    def stage1(index, step, g):
        start, piece, slot = piece_of(index)
        other = lax.rem(col + step, n_col)
        first = pl.multiple_of(g * out_rows + start + other * piece, 8)
        return pltpu.make_async_remote_copy(
            src_ref=part.at[pl.ds(first, piece)],
            dst_ref=mid.at[col * group + g, slot],
            send_sem=send1.at[index, step * group + g],
            recv_sem=recv1.at[index, step * group + g],
            device_id={"row": row, "col": other},
            device_id_type=MESH,
        )

    def arrive1(index, step, g):
        start, piece, slot = piece_of(index)
        other = lax.rem(col + n_col - step, n_col)
        pltpu.make_async_remote_copy(
            src_ref=part.at[pl.ds(start, piece)],
            dst_ref=mid.at[other * group + g, slot],
            send_sem=send1.at[index, step * group + g],
            recv_sem=recv1.at[index, step * group + g],
            device_id={"row": row, "col": other},
            device_id_type=MESH,
        ).wait_recv()

    def stage2(index, step):
        slot = piece_of(index)[2]
        other = lax.rem(row + step, n_row)
        return pltpu.make_async_remote_copy(
            src_ref=mid.at[other, slot],
            dst_ref=recv.at[step, slot],
            send_sem=send2.at[index, step],
            recv_sem=recv2.at[index, step],
            device_id={"row": other, "col": col},
            device_id_type=MESH,
        )

    def stage3(index, step):
        start, piece, _ = piece_of(index)
        here = out_ref.at[pl.ds(pl.multiple_of(start + col * piece, 8), piece)]
        return pltpu.make_async_remote_copy(
            src_ref=here,
            dst_ref=here,
            send_sem=send3.at[index, step],
            recv_sem=recv3.at[index, step],
            device_id={"row": row, "col": lax.rem(col + step, n_col)},
            device_id_type=MESH,
        )

    def arrive3(index, step):
        start, piece, _ = piece_of(index)
        other = lax.rem(col + n_col - step, n_col)
        there = out_ref.at[pl.ds(pl.multiple_of(start + other * piece, 8), piece)]
        pltpu.make_async_remote_copy(
            src_ref=there,
            dst_ref=there,
            send_sem=send3.at[index, step],
            recv_sem=recv3.at[index, step],
            device_id={"row": row, "col": other},
            device_id_type=MESH,
        ).wait_recv()

    def scatter(index):
        start, piece, slot = piece_of(index)
        for step in range(1, n_col):
            for g in range(group):
                stage1(index, step, g).start()
        for g in range(group):
            first = pl.multiple_of(g * out_rows + start + col * piece, 8)
            mid[col * group + g, slot] = part[pl.ds(first, piece)]

    def forward(index):
        for step in range(1, n_col):
            for g in range(group):
                arrive1(index, step, g)
        for step in range(1, n_row):
            stage2(index, step).start()

    def reduce(index):
        start, piece, slot = piece_of(index)
        total = mid[row, slot]
        for step in range(1, n_row):
            stage2(index, step).wait_recv()
            total = total + recv[step, slot]
        out_ref[pl.ds(pl.multiple_of(start + col * piece, 8), piece)] = total
        for step in range(1, n_col):
            stage3(index, step).start()

    for index, (start, rows) in enumerate(compute):
        here = pl.ds(start, rows)

        def multiply(t, _, index=index, here=here):
            deep = pl.ds(pl.multiple_of(t * deep_of(index), deep_of(index)), deep_of(index))
            load_a(index, t).wait()
            if index == 0:
                load_b(t).wait()
                high, low = split(b_ref[deep])
                if steps > 1:
                    b_high[deep] = high
                    b_low[deep] = low
            else:
                high, low = b_high[deep], b_low[deep]
            part[here] += product(a_ref[here, deep], high, low)
            return 0

        part[here] = jnp.zeros_like(part[here])
        turns = tiles if index == 0 else tiles // 2
        middle = turns // 2 if index > 0 else 0
        lax.fori_loop(0, middle, multiply, 0)
        if index > 0:
            for span in range((index - 1) * ratio, index * ratio):
                forward(span)
        lax.fori_loop(middle, turns, multiply, 0)
        if index == 0:
            pl.semaphore_wait(barrier, n_row + n_col - 2)
        for span in range(index * ratio, (index + 1) * ratio):
            scatter(span)
        if index > 0:
            for span in range((index - 1) * ratio, index * ratio):
                reduce(span)
    for span in range((steps - 1) * ratio, parts):
        forward(span)
    for span in range((steps - 1) * ratio, parts):
        reduce(span)
    for span in range(parts):
        for step in range(1, n_col):
            arrive3(span, step)
    for span in range(parts):
        for step in range(1, n_col):
            for g in range(group):
                stage1(span, step, g).wait_send()
            stage3(span, step).wait_send()
        for step in range(1, n_row):
            stage2(span, step).wait_send()


def shards(operator, basis):
    n_row = lax.axis_size("row")
    n_col = lax.axis_size("col")
    tile_rows, depth = operator.shape
    columns = basis.shape[1]
    group = n_row // n_col
    out_rows = tile_rows * n_col // n_row
    steps, parts = (COMPUTE, SPANS) if group == 1 else (1, 1)
    tile = min(TILE, depth)
    tiles = depth // tile
    dma = pltpu.SemaphoreType.DMA
    split_shape = (depth, columns) if steps > 1 else (16, columns)
    return pl.pallas_call(
        functools.partial(kernel, n_row, n_col, steps, parts, tile),
        out_shape=jax.ShapeDtypeStruct((out_rows, columns), jnp.float32),
        in_specs=[pl.BlockSpec(memory_space=pl.ANY)] * 2,
        out_specs=pl.BlockSpec(memory_space=pltpu.VMEM),
        scratch_shapes=[
            pltpu.VMEM((tile_rows, depth), jnp.float32),
            pltpu.VMEM((depth, columns), jnp.float32),
            pltpu.VMEM(split_shape, jnp.bfloat16),
            pltpu.VMEM(split_shape, jnp.bfloat16),
            pltpu.VMEM((tile_rows, columns), jnp.float32),
            pltpu.VMEM((n_row, out_rows // n_col, columns), jnp.float32),
            pltpu.VMEM((n_row, out_rows // n_col, columns), jnp.float32),
            dma((steps, tiles)),
            dma((tiles,)),
            dma((parts, n_row)),
            dma((parts, n_row)),
            dma((parts, n_row)),
            dma((parts, n_row)),
            dma((parts, n_col)),
            dma((parts, n_col)),
        ],
        compiler_params=pltpu.CompilerParams(
            collective_id=0, has_side_effects=True, vmem_limit_bytes=58 * 2**20
        ),
        cost_estimate=pl.CostEstimate(
            flops=6 * tile_rows * depth * columns,
            bytes_accessed=4 * (tile_rows * depth + depth * columns + out_rows * columns),
            transcendentals=0,
        ),
    )(operator, basis)


def solution(mesh):
    in_specs = (P(("reach", "col"), "row"), P(("reach", "row"), None))
    out_specs = P(("reach", "row"), None)
    return jax.shard_map(shards, mesh=mesh, in_specs=in_specs, out_specs=out_specs, check_vma=False)
```
